32 devices in a mesh: groups: 2 (over y), gx: 4 (over z), gy: 4 (over x, core).
Axes of the slice: x: 2, y: 2, z: 4, core: 2. Of those that a mesh axis runs over, the one named last changes fastest.
Arguments:
- tokens: bfloat16 [128, 16384], P(('groups', 'gy'), 'gx'), parts along dimension 0, may hold values from -6 to 6
- q_weight: bfloat16 [16384, 8192], P('gx', 'gy'), may hold values from -0.046875 to 0.046875
- k_weight: bfloat16 [16384, 512], P('gx', 'gy'), may hold values from -0.09375 to 0.09375
- v_weight: bfloat16 [16384, 512], P('gx', 'gy'), may hold values from -0.046875 to 0.046875
- out_weight: bfloat16 [8192, 16384], P('gy', 'gx'), may hold values from -0.0625 to 0.0625
- cache_keys: bfloat16 [16384, 512], P(('groups', 'gx'), 'gy'), parts along dimension 0, may hold values from -150 to 150
- cache_values: bfloat16 [16384, 512], P(('groups', 'gx'), 'gy'), parts along dimension 0, may hold values from -6 to 6
- tenant_ids: int32 [128], P('groups'), parts along dimension 0, may hold values from 0 to 7, never falling along the last dimension, each value on 1 to 16 neighbouring positions
- prefix_len: int32 [16], P('groups'), parts along dimension 0, may hold values from 1 to 8192, as said below
Outputs:
- mixed: bfloat16 [128, 16384], P(('groups', 'gy'), 'gx'), parts along dimension 0
The draws below stay inside these ranges and needn't reach their ends.
There are 2 independent parts, one for each index of `groups`. The reference program is written for one: setup_inputs(seed, part) draws one part's arguments, and reference() takes and returns one part's arrays. A program takes and returns all parts, laid end to end along the dimension named above; an argument that names none is the same for every part. Nothing has to cross between parts.
Inputs may be any that keep to these rules, and one draw needn't show every extreme that they name: `prefix_len`: some tenant reads all 8192 positions.
All inputs are finite; a program needn't handle non-finite values.
Results may differ from the reference program's by a relative error of at most 0.012.
Values may be sent and summed in bfloat16 or wider, within the bound.
A program may use at most 128 MiB of HBM per device.

```python
import math
import jax
import jax.numpy as jnp
import numpy as np
from jax import lax

D = 16384
QH = 64
KVH = 4
HD = 128
TOKENS = 64
TENANTS = 8
PREFIX = 8192


def planted_keys(base, spike_source, pick_key, strength_key, low, high):
    pair_count = 4
    starts = jax.random.randint(pick_key, (pair_count,), 0, max(1, PREFIX // 4), dtype=jnp.int32)
    stride_width = (high - low) / pair_count
    strengths = low + stride_width * (jnp.arange(pair_count, dtype=jnp.float32) + jax.random.uniform(strength_key, (pair_count,), jnp.float32))
    position = jnp.arange(PREFIX, dtype=jnp.int32)[:, None]
    matches = position == starts[None, :]
    picked = jnp.any(matches, axis=1, keepdims=True)
    strength = jnp.max(jnp.where(matches, strengths[None, :], 0.0), axis=1, keepdims=True)
    follows = jnp.roll(picked, 1, axis=0) & jnp.logical_not(picked)
    source = jnp.where(follows, jnp.roll(spike_source, 1, axis=0), jnp.where(picked, spike_source, base))
    factor = jnp.where(picked, strength, jnp.where(follows, 1.01 * jnp.roll(strength, 1, axis=0), 1.0))
    return source * factor


def draw_cache_keys(key, part):
    key = jax.random.fold_in(key, 11)
    base_key, pick_key, strength_key = jax.random.split(key, 3)
    unit = jnp.clip(jax.random.normal(base_key, (PREFIX, KVH * HD), jnp.float32), -6.0, 6.0)
    return planted_keys(3.0 * unit, jnp.clip(unit, -2.4, 2.4), pick_key, strength_key, 30.0, 60.0).astype(jnp.bfloat16)


def draw_prefix_len(key, part):
    key = jax.random.fold_in(key, 23)
    len_key, top_key = jax.random.split(key, 2)
    lengths = jax.random.randint(len_key, (TENANTS,), 1, PREFIX + 1, dtype=jnp.int32)
    longest = jax.random.randint(top_key, (), 0, TENANTS, dtype=jnp.int32)
    return jnp.where(jnp.arange(TENANTS, dtype=jnp.int32) == longest, PREFIX, lengths).astype(jnp.int32)


def shard_levels(stream_key, shape, pieces, least, top_value):
    gain, own = 1.0, jax.random.fold_in(stream_key, 6)
    for dim, shards_of in pieces:
        draws = jnp.exp(jax.random.uniform(jax.random.fold_in(own, dim), (shards_of,), jnp.float32, least / len(pieces), top_value / len(pieces)))
        gain = gain * jnp.repeat(draws, shape[dim] // shards_of).reshape([-1 if axis == dim else 1 for axis in range(len(shape))])
    return gain


def profile(count, total, limit, slope):
    loads = [(1 << 20) // math.isqrt(standing ** slope) + 1 for standing in range(2, count + 1)]
    spare, holding = total - limit - (count - 1), [1] * (count - 1)
    while spare > 0:
        free = [i for i in range(count - 1) if holding[i] < limit]
        mass, left = sum([loads[i] for i in free]), spare
        for i in free:
            extra = min(limit - holding[i], max(1, left * loads[i] // mass), spare)
            holding[i] = holding[i] + extra
            spare = spare - extra
    return np.array([limit] + holding)


def ragged(rng, amount, total, limit, slope):
    if amount == 2:
        one = jax.random.randint(rng, (), max(1, total - limit), min(limit, total - 1) + 1)
        return jnp.stack([one, total - one])
    sizes = jnp.asarray(profile(amount, total, limit, slope), jnp.int32)
    couples = (amount - 1) // 2
    giver, sink = sizes[1:1 + 2 * couples:2], sizes[2:2 + 2 * couples:2]
    room = jnp.minimum(giver - 1, limit - sink)
    passed = jax.random.randint(jax.random.fold_in(rng, 1), (couples,), 0, 1 << 20) % (room + 1)
    sizes = sizes.at[1:1 + 2 * couples:2].set(giver - passed).at[2:2 + 2 * couples:2].set(sink + passed)
    return sizes[jax.random.permutation(jax.random.fold_in(rng, 2), amount)]


def bell_draw(stream_key, extent, deviation, bound, cuts=(), kind=jnp.bfloat16):
    values = jax.random.normal(stream_key, extent, jnp.float32) * deviation
    if len(cuts) > 0:
        values = shard_levels(stream_key, extent, cuts, -0.22, 0.18) * values
    return jnp.clip(values, min=-bound, max=bound).astype(kind)


def setup_inputs(seed: int = 0, part: int = 0) -> dict:
    keys = jax.random.split(jax.random.key(seed), 10)
    own_keys = jax.random.split(jax.random.fold_in(keys[9], part), 10)
    return {
        "tokens": bell_draw(own_keys[0], (TOKENS, D), 1.0, 6.0, ((0, 4), (1, 4))),
        "q_weight": bell_draw(keys[1], (D, QH * HD), D ** -0.5, 0.046875, ((0, 4), (1, 4))),
        "k_weight": bell_draw(keys[2], (D, KVH * HD), (D // 4) ** -0.5, 0.09375, ((0, 4), (1, 4))),
        "v_weight": bell_draw(keys[3], (D, KVH * HD), D ** -0.5, 0.046875, ((0, 4), (1, 4))),
        "out_weight": bell_draw(keys[4], (QH * HD, D), (QH * HD) ** -0.5, 0.0625, ((0, 4), (1, 4))),
        "cache_keys": draw_cache_keys(jax.random.fold_in(jax.random.fold_in(keys[9], part), 71), part),
        "cache_values": bell_draw(own_keys[6], (PREFIX, KVH * HD), 1.0, 6.0, ((0, 4), (1, 4))),
        "tenant_ids": jnp.searchsorted(jnp.cumsum(ragged(own_keys[7], TENANTS, TOKENS, TOKENS // 4, 1)), jnp.arange(TOKENS), side="right").astype(jnp.int32),
        "prefix_len": draw_prefix_len(jax.random.fold_in(jax.random.fold_in(keys[9], part), 71), part),
    }


def reference(tokens, q_weight, k_weight, v_weight, out_weight, cache_keys, cache_values, tenant_ids, prefix_len):
    head_group = QH // KVH
    queries = jnp.dot(tokens, q_weight, preferred_element_type=jnp.float32).astype(jnp.bfloat16)
    new_keys = jnp.dot(tokens, k_weight, preferred_element_type=jnp.float32).astype(jnp.bfloat16)
    new_values = jnp.dot(tokens, v_weight, preferred_element_type=jnp.float32).astype(jnp.bfloat16)
    tenant_table = tenant_ids[:, None] == jnp.arange(TENANTS, dtype=jnp.int32)[None, :]
    prefix_of = lax.optimization_barrier(jnp.sum(jnp.where(tenant_table, prefix_len[None, :], 0), axis=1)).astype(jnp.int32)
    prefix_rows = jnp.repeat(prefix_of, head_group)
    token_pos = jnp.arange(TOKENS, dtype=jnp.int32)
    same_tenant = (tenant_ids[:, None] == tenant_ids[None, :]) & (token_pos[None, :] <= token_pos[:, None])
    same_rows = jnp.repeat(same_tenant, head_group, axis=0)
    key_block = math.gcd(PREFIX, 4096)
    score_scale = 1.0 / math.sqrt(HD)

    def head_attend(head):
        q_rows = lax.dynamic_slice_in_dim(queries, head * head_group * HD, head_group * HD, 1).reshape(TOKENS * head_group, HD)
        keys_head = lax.dynamic_slice_in_dim(cache_keys, head * HD, HD, 1)
        values_head = lax.dynamic_slice_in_dim(cache_values, head * HD, HD, 1)
        fresh_keys = lax.dynamic_slice_in_dim(new_keys, head * HD, HD, 1)
        fresh_values = lax.dynamic_slice_in_dim(new_values, head * HD, HD, 1)
        fresh_scores = jnp.dot(q_rows, fresh_keys.T, preferred_element_type=jnp.float32) * score_scale
        row_peak = lax.optimization_barrier(jnp.max(jnp.where(same_rows, fresh_scores, -1e+30), axis=1))
        fresh_weights = jnp.where(same_rows, jnp.exp(fresh_scores - row_peak[:, None]), 0.0).astype(jnp.bfloat16)
        row_total = lax.optimization_barrier(jnp.sum(fresh_weights.astype(jnp.float32), axis=1))
        row_acc = jnp.dot(fresh_weights, fresh_values, preferred_element_type=jnp.float32)

        def scan_step(carry, block_index):
            old_peak, old_total, old_acc = carry
            key_slab = lax.dynamic_slice_in_dim(keys_head, block_index * key_block, key_block, 0)
            value_slab = lax.dynamic_slice_in_dim(values_head, block_index * key_block, key_block, 0)
            slab_scores = jnp.dot(q_rows, key_slab.T, preferred_element_type=jnp.float32) * score_scale
            key_pos = block_index * key_block + jnp.arange(key_block, dtype=jnp.int32)
            allowed = key_pos[None, :] < prefix_rows[:, None]
            new_peak = jnp.maximum(old_peak, lax.optimization_barrier(jnp.max(jnp.where(allowed, slab_scores, -1e+30), axis=1)))
            slab_weights = jnp.where(allowed, jnp.exp(slab_scores - new_peak[:, None]), 0.0).astype(jnp.bfloat16)
            rescale = jnp.exp(old_peak - new_peak)
            new_total = old_total * rescale + lax.optimization_barrier(jnp.sum(slab_weights.astype(jnp.float32), axis=1))
            new_acc = old_acc * rescale[:, None] + jnp.dot(slab_weights, value_slab, preferred_element_type=jnp.float32)
            return ((new_peak, new_total, new_acc), None)
        carry, _ = lax.scan(scan_step, (row_peak, row_total, row_acc), jnp.arange(PREFIX // key_block, dtype=jnp.int32))
        final_total = carry[1]
        final_acc = carry[2]
        return (final_acc / final_total[:, None]).astype(jnp.bfloat16).reshape(TOKENS, head_group * HD)
    head_outputs = lax.map(head_attend, jnp.arange(KVH, dtype=jnp.int32))
    attended = jnp.transpose(head_outputs, (1, 0, 2)).reshape(TOKENS, QH * HD)
    return jnp.dot(attended, out_weight, preferred_element_type=jnp.float32).astype(jnp.bfloat16)
```

```python
import functools
import math

import jax
import jax.numpy as jnp
from jax import lax
from jax.experimental import pallas as pl
from jax.experimental.pallas import tpu as pltpu
from jax.sharding import PartitionSpec as P

BF = jnp.bfloat16
F32 = jnp.float32
WIRE = jnp.float32
TILE = 256
ROWS = 16


def fused(
    nx,
    ny,
    heads,
    hd,
    hpg,
    tokens,
    q_weight,
    k_weight,
    v_weight,
    out_weight,
    cache_keys,
    cache_values,
    tenants,
    prefix_len,
    out,
    tok_full,
    wq,
    wkv,
    wo,
    kbuf,
    vbuf,
    vones,
    bias,
    part,
    wire,
    recv_end,
    recv_mid,
    fresh,
    q_full,
    scores,
    o_part,
    l_part,
    o_wire,
    l_wire,
    o_end,
    l_end,
    o_mid,
    l_mid,
    att_full,
    macc,
    o2_send,
    recv3,
    pair_sum,
    recv4,
    load_sem,
    tok_sem,
    up_sem,
    across_sem,
    down_sem,
    o_up_sem,
    o_across_sem,
    l_up_sem,
    l_across_sem,
    o_down_sem,
    r3_sem,
    r4_sem,
):
    ix = lax.axis_index("gx")
    iy = lax.axis_index("gy")
    width = heads * hd
    groups = heads // hpg
    gw = hpg * hd
    total = nx * ROWS
    cache_rows = cache_keys.shape[0]
    scale = math.log2(math.e) / math.sqrt(hd)

    def load(src, dst, i):
        copy = pltpu.make_async_copy(src, dst, load_sem.at[i])
        copy.start()
        return copy

    end = (ix == 0) | (ix == nx - 1)
    mid = jnp.logical_not(end)
    inner = jnp.where(ix == 0, 1, nx - 2)
    outer = jnp.where(ix == 1, 0, nx - 1)
    other = nx - 1 - ix
    core = lax.rem(iy, 2)
    cell = iy // 2
    sibling = iy + 1 - 2 * core
    across = lax.rem(iy + 2, ny)

    def remote(src, dst, sems, axis, target):
        return pltpu.make_async_remote_copy(
            src_ref=src,
            dst_ref=dst,
            send_sem=sems.at[0],
            recv_sem=sems.at[1],
            device_id={axis: target},
            device_id_type=pl.DeviceIdType.MESH,
        )

    def signal(axis, target):
        pl.semaphore_signal(
            barrier, inc=1, device_id={axis: target}, device_id_type=pl.DeviceIdType.MESH
        )

    own_tokens = load(tokens, tok_full.at[iy], 0)
    wk_copy = load(k_weight, wkv.at[:, :hd], 1)
    wv_copy = load(v_weight, wkv.at[:, hd:], 2)
    wq_copies = [
        load(q_weight.at[:, pl.ds(c * gw, gw)], wq.at[:, pl.ds(c * gw, gw)], 3 + c)
        for c in range(groups)
    ]
    key_copy = load(cache_keys, kbuf.at[pl.ds(0, cache_rows)], 3 + groups)
    value_copy = load(cache_values, vbuf.at[pl.ds(0, cache_rows)], 4 + groups)

    barrier = pltpu.get_barrier_semaphore()
    signal("gy", sibling)
    signal("gy", across)

    @pl.when(end)
    def _():
        signal("gx", inner)
        pl.semaphore_wait(barrier, 3)

    @pl.when(mid)
    def _():
        signal("gx", outer)
        signal("gx", other)
        pl.semaphore_wait(barrier, 4)

    tok_across = remote(tokens, tok_full.at[iy], tok_sem.at[0], "gy", across)
    tok_across.start()
    tok_pair = remote(tokens, tok_full.at[iy], tok_sem.at[1], "gy", sibling)
    tok_pair.start()

    tid_row = tenants[...].astype(F32)
    r = lax.broadcasted_iota(jnp.int32, (total, total), 0)
    l = lax.broadcasted_iota(jnp.int32, (total, total), 1)
    tid = jnp.sum(
        jnp.where(r == l, jnp.broadcast_to(tid_row, (total, total)), 0.0), axis=1, keepdims=True
    )
    reach = jnp.zeros((total, 1), jnp.int32)
    for i in range(prefix_len.shape[0]):
        reach = jnp.where(tid == float(i), prefix_len[i], reach)
    pos = lax.broadcasted_iota(jnp.int32, (total, cache_rows), 1) + ix * cache_rows
    bias[:, pl.ds(0, cache_rows)] = jnp.where(pos < reach, 0.0, -1e30)
    row = lax.broadcasted_iota(jnp.int32, (total, 128), 0)
    lane = lax.broadcasted_iota(jnp.int32, (total, 128), 1)
    half = total // 2
    new = lane + (ix - 1) * half
    new_tid = jnp.sum(jnp.where(row == new, tid, 0.0), axis=0, keepdims=True)
    ok = (new_tid == tid) & (new <= row) & (lane < half) & (new >= 0)
    bias[:, pl.ds(cache_rows, 128)] = jnp.where(ok, 0.0, -1e30)
    vones[...] = jnp.ones_like(vones)
    kbuf[pl.ds(cache_rows, 128), :] = jnp.zeros((128, hd), BF)
    vbuf[pl.ds(cache_rows, 128), :] = jnp.zeros((128, hd), BF)

    wo_copies = []
    eye = row == lane
    level = lax.broadcasted_iota(jnp.int32, (8, 128), 0)

    def to_lanes(columns):
        tile = jnp.zeros((8, 128), F32)
        for h, column in enumerate(columns):
            flat = jnp.sum(jnp.where(eye, column, 0.0), axis=0, keepdims=True)
            tile = jnp.where(level == h, flat, tile)
        return tile

    def from_lanes(tile, h):
        return jnp.sum(jnp.where(eye, tile[h : h + 1, :], 0.0), axis=1, keepdims=True)

    def span_of(c):
        return pl.ds(c * gw, gw if c < groups else 2 * hd)

    def up(c):
        return remote(wire.at[:, span_of(c)], recv_end.at[:, span_of(c)], up_sem.at[c], "gx", inner)

    def over(c):
        return remote(wire.at[:, span_of(c)], recv_mid.at[:, span_of(c)], across_sem.at[c], "gx", other)

    def down(c):
        return remote(q_full.at[:, span_of(c)], q_full.at[:, span_of(c)], down_sem.at[c], "gx", outer)

    def o_up(c):
        return (
            remote(l_wire.at[c], l_end.at[c], l_up_sem.at[c], "gx", inner),
            remote(o_wire.at[c], o_end.at[c], o_up_sem.at[c], "gx", inner),
        )

    def o_over(c):
        return (
            remote(l_wire.at[c], l_mid.at[c], l_across_sem.at[c], "gx", other),
            remote(o_wire.at[c], o_mid.at[c], o_across_sem.at[c], "gx", other),
        )

    def o_down(c):
        return remote(
            att_full.at[:, span_of(c)], att_full.at[:, span_of(c)], o_down_sem.at[c], "gx", outer
        )

    def project(c):
        base = c * gw
        span = gw if c < groups else 2 * hd
        if c < groups:
            wq_copies[c].wait()
            wo_copies.append(
                load(out_weight.at[pl.ds(base, gw)], wo.at[pl.ds(base, gw)], 5 + groups + c)
            )
        else:
            wk_copy.wait()
            wv_copy.wait()

        @pl.loop(0, span // TILE)
        def _(i):
            at = pl.multiple_of(i * TILE, TILE)
            w = wq[:, pl.ds(base + at, TILE)] if c < groups else wkv[:, pl.ds(at, TILE)]
            y = jnp.dot(
                tok_full[...].reshape(total, -1), w, preferred_element_type=F32
            )
            part[:, pl.ds(base + at, TILE)] = y

            @pl.when(end)
            def _():
                wire[:, pl.ds(base + at, TILE)] = y.astype(WIRE)

        @pl.when(end)
        def _():
            up(c).start()

    def pass_on(c):
        @pl.when(mid)
        def _():
            up(c).wait_recv()
            cols = span_of(c)
            y = part[:, cols] + recv_end[:, cols].astype(F32)
            part[:, cols] = y
            wire[:, cols] = y.astype(WIRE)
            over(c).start()

    def settle(c):
        if c == groups:
            key_copy.wait()
            value_copy.wait()

        @pl.when(mid)
        def _():
            over(c).wait_recv()
            cols = span_of(c)
            y = (part[:, cols] + recv_mid[:, cols].astype(F32)).astype(BF)
            if c == groups:
                fresh[...] = y.reshape(2, half, 2 * hd)
                own = fresh[ix - 1]
                kbuf[pl.ds(cache_rows, half), :] = own[:, :hd]
                vbuf[pl.ds(cache_rows, half), :] = own[:, hd:]
            else:
                q_full[:, cols] = y
                down(c).start()

    tiles = [(a, min(512, cache_rows - a)) for a in range(0, cache_rows, 512)]
    tiles.append((cache_rows, 128))

    def attend(c):
        @pl.when(end)
        def _():
            down(c).wait_recv()

        q = jnp.concatenate(
            [
                q_full[:, pl.ds(c * gw + h * hd, hd)]
                for h in range(hpg)
            ],
            axis=0,
        )
        peak = jnp.full((hpg * total, 1), -1e20, F32)
        for a, t in tiles:
            s = lax.dot_general(
                q,
                kbuf[pl.ds(a, t), :],
                (((1,), (1,)), ((), ())),
                preferred_element_type=F32,
            )
            s = (s * scale).reshape(hpg, total, t) + bias[:, pl.ds(a, t)][None]
            s = s.reshape(hpg * total, t)
            scores[:, pl.ds(a, t)] = s
            peak = jnp.maximum(peak, jnp.max(s, axis=1, keepdims=True))
        acc = jnp.zeros((hpg * total, 2 * hd), F32)
        for a, t in tiles:
            p = jnp.exp2(scores[:, pl.ds(a, t)] - peak).astype(BF)
            v = jnp.concatenate([vbuf[pl.ds(a, t), :], vones[pl.ds(0, t), :]], axis=1)
            acc = acc + jnp.dot(p, v, preferred_element_type=F32)
        norm = acc[:, hd : hd + 1]
        some = norm > 0.0
        o = acc[:, :hd] / jnp.where(some, norm, 1.0)
        lse = jnp.where(some, peak + jnp.log2(jnp.where(some, norm, 1.0)), -1e20)
        parts = [slice(h * total, (h + 1) * total) for h in range(hpg)]
        tile = to_lanes([lse[rows] for rows in parts])
        wide = jnp.concatenate([o[rows] for rows in parts], axis=1)

        @pl.when(end)
        def _():
            l_wire[c] = tile
            o_wire[c] = wide.astype(BF)
            for copy in o_up(c):
                copy.start()

        @pl.when(mid)
        def _():
            l_part[c] = tile
            o_part[c] = wide

    def merged(c, o_ref, l_ref):
        mine, theirs = l_part[c], l_ref[c]
        top = jnp.maximum(mine, theirs)
        left, right = jnp.exp2(mine - top), jnp.exp2(theirs - top)
        both = left + right
        left, right = left / both, right / both
        pieces = []
        for h in range(hpg):
            cols = pl.ds(h * hd, hd)
            pieces.append(
                o_part[c, :, cols] * from_lanes(left, h)
                + o_ref[c, :, cols].astype(F32) * from_lanes(right, h)
            )
        return jnp.concatenate(pieces, axis=1), top + jnp.log2(both)

    def merge(c):
        @pl.when(mid)
        def _():
            for copy in o_up(c):
                copy.wait_recv()
            wide, tile = merged(c, o_end, l_end)
            l_part[c] = tile
            o_part[c] = wide
            l_wire[c] = tile
            o_wire[c] = wide.astype(BF)
            for copy in o_over(c):
                copy.start()

    def finish(c):
        @pl.when(mid)
        def _():
            for copy in o_over(c):
                copy.wait_recv()
            wide, _ = merged(c, o_mid, l_mid)
            att_full[:, span_of(c)] = wide.astype(BF)
            o_down(c).start()

    out_cols = out.shape[1]
    spans = 4
    sw = out_cols // spans

    def pair_copy(n):
        cols = pl.ds(n * sw, sw)
        return remote(
            o2_send.at[:, 1 - core, :, cols], recv3.at[:, :, cols], r3_sem.at[n], "gy", sibling
        )

    def cell_copy(n):
        cols = pl.ds(n * sw, sw)
        return remote(pair_sum.at[:, cols], recv4.at[:, cols], r4_sem.at[n], "gy", across)

    def pair(n):
        cols = pl.ds(n * sw, sw)
        pair_copy(n).wait_recv()
        y = o2_send[1 - cell, core, :, cols].astype(F32) + recv3[1 - cell, :, cols].astype(F32)
        pair_sum[:, cols] = y.astype(BF)
        cell_copy(n).start()


    def mix(c):
        @pl.when(end)
        def _():
            o_down(c).wait_recv()

        wo_copies[c].wait()
        last = c == groups - 1

        def columns(at):
            a = att_full[:, pl.ds(c * gw, gw)]
            y = jnp.dot(
                a, wo[pl.ds(c * gw, gw), pl.ds(at, TILE)], preferred_element_type=F32
            )
            if c > 0:
                y = y + macc[:, pl.ds(at, TILE)]
            if last:
                o2_send[:, :, :, pl.ds(at, TILE)] = y.astype(BF).reshape(2, 2, ROWS, TILE)
            else:
                macc[:, pl.ds(at, TILE)] = y

        if not last:

            @pl.loop(0, out_cols // TILE)
            def _(i):
                columns(pl.multiple_of(i * TILE, TILE))

            return
        for n in range(spans):

            @pl.loop(0, sw // TILE)
            def _(i):
                columns(pl.multiple_of(n * sw + i * TILE, TILE))

            pair_copy(n).start()
            if n > 0:
                pair(n - 1)
        pair(spans - 1)

    own_tokens.wait()
    tok_across.wait_recv()
    tok_relay = remote(tok_full.at[across], tok_full.at[across], tok_sem.at[2], "gy", sibling)
    tok_relay.start()
    tok_pair.wait_recv()
    tok_relay.wait_recv()
    steps = ('Pk', 'P0', 'P1', 'Xk', 'P2', 'X0', 'P3', 'X1', 'Yk', 'Y0', 'X2', 'Y1', 'X3', 'A0', 'Y2', 'A1', 'Y3', 'A2', 'A3', 'U0', 'U1', 'V0', 'U2', 'V1', 'M0', 'U3', 'V2', 'M1', 'V3', 'M2', 'M3')
    table = dict(P=project, X=pass_on, Y=settle, A=attend, U=merge, V=finish, M=mix)
    for step in steps:
        table[step[0]](groups if step[1] == "k" else int(step[1]))

    for n in range(spans):
        cols = pl.ds(n * sw, sw)
        y = o2_send[cell, core, :, cols].astype(F32) + recv3[cell, :, cols].astype(F32)
        cell_copy(n).wait_recv()
        out[:, cols] = (y + recv4[:, cols].astype(F32)).astype(BF)

    tok_across.wait_send()
    tok_pair.wait_send()
    tok_relay.wait_send()
    for n in range(spans):
        pair_copy(n).wait_send()
        cell_copy(n).wait_send()

    @pl.when(end)
    def _():
        for c in range(groups + 1):
            up(c).wait_send()
        for c in range(groups):
            for copy in o_up(c):
                copy.wait_send()

    @pl.when(mid)
    def _():
        for c in range(groups + 1):
            over(c).wait_send()
        for c in range(groups):
            down(c).wait_send()
            o_down(c).wait_send()
            for copy in o_over(c):
                copy.wait_send()


def fused_body(nx, ny, *args):
    tokens, q_weight, k_weight, v_weight, out_weight, cache_keys, cache_values, tenant_ids, prefix_len = args
    hd = cache_keys.shape[1]
    width = q_weight.shape[1]
    heads = width // hd
    groups = 4
    hpg = heads // groups
    gw = hpg * hd
    total = tenant_ids.shape[0]
    depth = tokens.shape[1]
    out_cols = out_weight.shape[1]
    rows = cache_keys.shape[0] + 128
    anywhere = pl.BlockSpec(memory_space=pl.ANY)
    vmem = pl.BlockSpec(memory_space=pltpu.VMEM)
    dma = pltpu.SemaphoreType.DMA
    chunks = groups + 1
    return pl.pallas_call(
        functools.partial(fused, nx, ny, heads, hd, hpg),
        out_shape=jax.ShapeDtypeStruct((ROWS, out_cols), BF),
        in_specs=[anywhere] * 7 + [vmem, pl.BlockSpec(memory_space=pltpu.SMEM)],
        out_specs=vmem,
        scratch_shapes=[
            pltpu.VMEM((ny, ROWS, depth), BF),
            pltpu.VMEM((depth, width), BF),
            pltpu.VMEM((depth, 2 * hd), BF),
            pltpu.VMEM((width, out_cols), BF),
            pltpu.VMEM((rows, hd), BF),
            pltpu.VMEM((rows, hd), BF),
            pltpu.VMEM((512, hd), BF),
            pltpu.VMEM((total, rows), F32),
            pltpu.VMEM((total, width + 2 * hd), F32),
            pltpu.VMEM((total, width + 2 * hd), WIRE),
            pltpu.VMEM((total, width + 2 * hd), WIRE),
            pltpu.VMEM((total, width + 2 * hd), WIRE),
            pltpu.VMEM((2, total // 2, 2 * hd), BF),
            pltpu.VMEM((total, width), BF),
            pltpu.VMEM((hpg * total, rows), F32),
            pltpu.VMEM((groups, total, gw), F32),
            pltpu.VMEM((groups, 8, 128), F32),
            pltpu.VMEM((groups, total, gw), BF),
            pltpu.VMEM((groups, 8, 128), F32),
            pltpu.VMEM((groups, total, gw), BF),
            pltpu.VMEM((groups, 8, 128), F32),
            pltpu.VMEM((groups, total, gw), BF),
            pltpu.VMEM((groups, 8, 128), F32),
            pltpu.VMEM((total, width), BF),
            pltpu.VMEM((total, out_cols), F32),
            pltpu.VMEM((2, 2, ROWS, out_cols), BF),
            pltpu.VMEM((2, ROWS, out_cols), BF),
            pltpu.VMEM((ROWS, out_cols), BF),
            pltpu.VMEM((ROWS, out_cols), BF),
            dma((5 + 2 * groups,)),
            dma((3, 2)),
            dma((chunks, 2)),
            dma((chunks, 2)),
            dma((groups, 2)),
            dma((groups, 2)),
            dma((groups, 2)),
            dma((groups, 2)),
            dma((groups, 2)),
            dma((groups, 2)),
            dma((4, 2)),
            dma((4, 2)),
        ],
        compiler_params=pltpu.CompilerParams(
            collective_id=0, has_side_effects=True, vmem_limit_bytes=56 * 2**20
        ),
    )(
        tokens,
        q_weight,
        k_weight,
        v_weight,
        out_weight,
        cache_keys,
        cache_values,
        tenant_ids.reshape(1, total),
        prefix_len,
    )


def joined(part, axis, combine):
    gathered = jax.tree.map(lambda a: lax.all_gather(a, axis), part)

    def take(source):
        return jax.tree.map(lambda a: lax.dynamic_index_in_dim(a, source, 0, False), gathered)

    return lax.fori_loop(
        1, lax.axis_size(axis), lambda source, state: combine(state, take(source)), take(0)
    )


def combine_parts(left_part, right_part):
    left_peak, left_total, left_acc = left_part
    right_peak, right_total, right_acc = right_part
    joint_peak = jnp.maximum(left_peak, right_peak)
    left_factor = jnp.exp(left_peak - joint_peak)
    right_factor = jnp.exp(right_peak - joint_peak)
    joint_total = left_total * left_factor + right_total * right_factor
    joint_acc = left_acc * left_factor[..., None] + right_acc * right_factor[..., None]
    return (joint_peak, joint_total, joint_acc)


def body(
    tokens,
    q_weight,
    k_weight,
    v_weight,
    out_weight,
    cache_keys,
    cache_values,
    tenant_ids,
    prefix_len,
):
    head_dim = cache_keys.shape[1]
    q_width = q_weight.shape[1]
    head_group = q_width // head_dim
    total_tokens = tenant_ids.shape[0]
    own_rows = total_tokens // lax.axis_size("gx")
    gathered = lax.all_gather(tokens, "gy", axis=0, tiled=True)
    slab_rows = gathered
    projected = lax.psum_scatter(
        jnp.concatenate(
            [
                jnp.dot(slab_rows, q_weight, preferred_element_type=jnp.float32),
                jnp.dot(slab_rows, k_weight, preferred_element_type=jnp.float32),
                jnp.dot(slab_rows, v_weight, preferred_element_type=jnp.float32),
            ],
            axis=1,
        ),
        "gx",
        scatter_dimension=0,
        tiled=True,
    )
    own_queries = projected[:, :q_width].astype(jnp.bfloat16)
    new_keys = projected[:, q_width : q_width + head_dim].astype(jnp.bfloat16)
    new_values = projected[:, q_width + head_dim :].astype(jnp.bfloat16)
    queries = lax.all_gather(own_queries, "gx", axis=0, tiled=True)
    device_index = lax.axis_index("gx")
    tenant_count = prefix_len.shape[0]
    tenant_table = tenant_ids[:, None] == jnp.arange(tenant_count, dtype=jnp.int32)[None, :]
    prefix_of = jnp.sum(jnp.where(tenant_table, prefix_len[None, :], 0), axis=1)
    cache_rows = cache_keys.shape[0]
    key_pos = device_index * cache_rows + jnp.arange(cache_rows, dtype=jnp.int32)
    new_pos = device_index * own_rows + jnp.arange(own_rows, dtype=jnp.int32)
    new_tenant = lax.dynamic_slice_in_dim(tenant_ids, device_index * own_rows, own_rows, 0)
    block_tokens = math.gcd(total_tokens, max(1, 512 // head_group))
    score_scale = 1.0 / math.sqrt(head_dim)

    def attend_block(block_index):
        first_token = block_index * block_tokens
        q_rows = lax.dynamic_slice_in_dim(queries, first_token, block_tokens, 0).reshape(
            block_tokens * head_group, head_dim
        )
        rows_prefix = jnp.repeat(
            lax.dynamic_slice_in_dim(prefix_of, first_token, block_tokens, 0), head_group
        )
        rows_tenant = jnp.repeat(
            lax.dynamic_slice_in_dim(tenant_ids, first_token, block_tokens, 0), head_group
        )
        rows_pos = jnp.repeat(first_token + jnp.arange(block_tokens, dtype=jnp.int32), head_group)
        prefix_scores = (
            jnp.dot(q_rows, cache_keys.T, preferred_element_type=jnp.float32) * score_scale
        )
        allowed_prefix = key_pos[None, :] < rows_prefix[:, None]
        fresh_scores = jnp.dot(q_rows, new_keys.T, preferred_element_type=jnp.float32) * score_scale
        allowed_fresh = (new_tenant[None, :] == rows_tenant[:, None]) & (
            new_pos[None, :] <= rows_pos[:, None]
        )
        row_peak = jnp.maximum(
            jnp.max(jnp.where(allowed_prefix, prefix_scores, -1e30), axis=1),
            jnp.max(jnp.where(allowed_fresh, fresh_scores, -1e30), axis=1),
        )
        prefix_weights = jnp.where(
            allowed_prefix, jnp.exp(prefix_scores - row_peak[:, None]), 0.0
        ).astype(jnp.bfloat16)
        fresh_weights = jnp.where(
            allowed_fresh, jnp.exp(fresh_scores - row_peak[:, None]), 0.0
        ).astype(jnp.bfloat16)
        row_total = jnp.sum(prefix_weights.astype(jnp.float32), axis=1) + jnp.sum(
            fresh_weights.astype(jnp.float32), axis=1
        )
        row_acc = jnp.dot(prefix_weights, cache_values, preferred_element_type=jnp.float32)
        row_acc = row_acc + jnp.dot(fresh_weights, new_values, preferred_element_type=jnp.float32)
        return (
            row_peak.reshape(block_tokens, head_group),
            row_total.reshape(block_tokens, head_group),
            row_acc.reshape(block_tokens, head_group, head_dim),
        )

    peak_blocks, total_blocks, acc_blocks = lax.map(
        attend_block, jnp.arange(total_tokens // block_tokens, dtype=jnp.int32)
    )
    row_peaks = peak_blocks.reshape(total_tokens, head_group)
    row_totals = total_blocks.reshape(total_tokens, head_group)
    row_accs = acc_blocks.reshape(total_tokens, head_group, head_dim)
    joint_peak, joint_total, joint_acc = joined(
        (row_peaks, row_totals, row_accs), "gx", combine_parts
    )
    attended = (
        (joint_acc / joint_total[..., None]).astype(jnp.bfloat16).reshape(total_tokens, q_width)
    )
    slab_rows = attended
    mixed = lax.psum_scatter(
        jnp.dot(slab_rows, out_weight, preferred_element_type=jnp.float32),
        "gy",
        scatter_dimension=0,
        tiled=True,
    )
    return mixed.astype(jnp.bfloat16)


def solution(mesh):
    placed = (
        P(("groups", "gy"), "gx"),
        P("gx", "gy"),
        P("gx", "gy"),
        P("gx", "gy"),
        P("gy", "gx"),
        P(("groups", "gx"), "gy"),
        P(("groups", "gx"), "gy"),
        P("groups"),
        P("groups"),
    )
    nx, ny = mesh.shape["gx"], mesh.shape["gy"]

    def local(*args):
        whole = args[7].shape[0]
        if nx == ny == 4 and whole == nx * ROWS:
            return fused_body(nx, ny, *args)
        return body(*args)

    return jax.shard_map(
        local, mesh=mesh, in_specs=placed, out_specs=P(("groups", "gy"), "gx"), check_vma=False
    )
```

```python
import functools
import math

import jax
import jax.numpy as jnp
from jax import lax
from jax.experimental import pallas as pl
from jax.experimental.pallas import tpu as pltpu
from jax.sharding import PartitionSpec as P

BF = jnp.bfloat16
F32 = jnp.float32
I16 = jnp.int16
TILE = 1024
ROWS = 16
LEVELS = 32000.0


def fused(
    nx,
    ny,
    heads,
    hd,
    hpg,
    tokens,
    q_weight,
    k_weight,
    v_weight,
    out_weight,
    cache_keys,
    cache_values,
    tenants,
    prefix_len,
    out,
    tok_full,
    wq,
    wkv,
    wo,
    kbuf,
    vbuf,
    vones,
    bias,
    part,
    wire,
    recv_end,
    recv_mid,
    s_wire,
    s_end,
    s_mid,
    fresh,
    q_full,
    scores,
    o_part,
    l_part,
    o_wire,
    l_wire,
    o_end,
    l_end,
    o_mid,
    l_mid,
    att_full,
    macc,
    o2_send,
    recv3,
    pair_sum,
    recv4,
    load_sem,
    tok_sem,
    up_sem,
    across_sem,
    s_up_sem,
    s_across_sem,
    down_sem,
    o_up_sem,
    o_across_sem,
    l_up_sem,
    l_across_sem,
    o_down_sem,
    r3_sem,
    r4_sem,
):
    ix = lax.axis_index("gx")
    iy = lax.axis_index("gy")
    width = heads * hd
    groups = heads // hpg
    gw = hpg * hd
    total = nx * ROWS
    cache_rows = cache_keys.shape[0]
    scale = math.log2(math.e) / math.sqrt(hd)

    def load(src, dst, i):
        copy = pltpu.make_async_copy(src, dst, load_sem.at[i])
        copy.start()
        return copy

    end = (ix == 0) | (ix == nx - 1)
    mid = jnp.logical_not(end)
    inner = jnp.where(ix == 0, 1, nx - 2)
    outer = jnp.where(ix == 1, 0, nx - 1)
    other = nx - 1 - ix
    core = lax.rem(iy, 2)
    cell = iy // 2
    sibling = iy + 1 - 2 * core
    across = lax.rem(iy + 2, ny)

    def remote(src, dst, sems, axis, target):
        return pltpu.make_async_remote_copy(
            src_ref=src,
            dst_ref=dst,
            send_sem=sems.at[0],
            recv_sem=sems.at[1],
            device_id={axis: target},
            device_id_type=pl.DeviceIdType.MESH,
        )

    def signal(axis, target):
        pl.semaphore_signal(
            barrier, inc=1, device_id={axis: target}, device_id_type=pl.DeviceIdType.MESH
        )

    own_tokens = load(tokens, tok_full.at[iy], 0)
    wk_copy = load(k_weight, wkv.at[:, :hd], 1)
    wv_copy = load(v_weight, wkv.at[:, hd:], 2)
    wq_copies = [
        load(q_weight.at[:, pl.ds(c * gw, gw)], wq.at[:, pl.ds(c * gw, gw)], 3 + c)
        for c in range(groups)
    ]
    key_copy = load(cache_keys, kbuf.at[pl.ds(0, cache_rows)], 3 + groups)
    value_copy = load(cache_values, vbuf.at[pl.ds(0, cache_rows)], 4 + groups)

    barrier = pltpu.get_barrier_semaphore()
    signal("gy", sibling)
    signal("gy", across)

    @pl.when(end)
    def _():
        signal("gx", inner)
        pl.semaphore_wait(barrier, 3)

    @pl.when(mid)
    def _():
        signal("gx", outer)
        signal("gx", other)
        pl.semaphore_wait(barrier, 4)

    tok_across = remote(tokens, tok_full.at[iy], tok_sem.at[0], "gy", across)
    tok_across.start()
    tok_pair = remote(tokens, tok_full.at[iy], tok_sem.at[1], "gy", sibling)
    tok_pair.start()

    tid_row = tenants[...].astype(F32)
    r = lax.broadcasted_iota(jnp.int32, (total, total), 0)
    l = lax.broadcasted_iota(jnp.int32, (total, total), 1)
    tid = jnp.sum(
        jnp.where(r == l, jnp.broadcast_to(tid_row, (total, total)), 0.0), axis=1, keepdims=True
    )
    reach = jnp.zeros((total, 1), jnp.int32)
    for i in range(prefix_len.shape[0]):
        reach = jnp.where(tid == float(i), prefix_len[i], reach)
    pos = lax.broadcasted_iota(jnp.int32, (total, cache_rows), 1) + ix * cache_rows
    bias[:, pl.ds(0, cache_rows)] = jnp.where(pos < reach, 0.0, -1e30)
    row = lax.broadcasted_iota(jnp.int32, (total, 128), 0)
    lane = lax.broadcasted_iota(jnp.int32, (total, 128), 1)
    half = total // 2
    new = lane + (ix - 1) * half
    new_tid = jnp.sum(jnp.where(row == new, tid, 0.0), axis=0, keepdims=True)
    ok = (new_tid == tid) & (new <= row) & (lane < half) & (new >= 0)
    bias[:, pl.ds(cache_rows, 128)] = jnp.where(ok, 0.0, -1e30)
    vones[...] = jnp.ones_like(vones)
    kbuf[pl.ds(cache_rows, 128), :] = jnp.zeros((128, hd), BF)
    vbuf[pl.ds(cache_rows, 128), :] = jnp.zeros((128, hd), BF)

    wo_copies = []
    eye = row == lane
    level = lax.broadcasted_iota(jnp.int32, (8, 128), 0)

    def to_lanes(columns):
        tile = jnp.zeros((8, 128), F32)
        for h, column in enumerate(columns):
            flat = jnp.sum(jnp.where(eye, column, 0.0), axis=0, keepdims=True)
            tile = jnp.where(level == h, flat, tile)
        return tile

    def from_lanes(tile, h):
        return jnp.sum(jnp.where(eye, tile[h : h + 1, :], 0.0), axis=1, keepdims=True)

    def span_of(c):
        return pl.ds(c * gw, gw if c < groups else 2 * hd)

    def up(c):
        return (
            remote(s_wire.at[c], s_end.at[c], s_up_sem.at[c], "gx", inner),
            remote(wire.at[:, span_of(c)], recv_end.at[:, span_of(c)], up_sem.at[c], "gx", inner),
        )

    def over(c):
        return (
            remote(s_wire.at[c], s_mid.at[c], s_across_sem.at[c], "gx", other),
            remote(
                wire.at[:, span_of(c)], recv_mid.at[:, span_of(c)], across_sem.at[c], "gx", other
            ),
        )

    def heads_of(c):
        return hpg if c < groups else 2

    def encode(c, y):
        steps = []
        for h in range(heads_of(c)):
            z = y[:, h * hd : (h + 1) * hd]
            top = jnp.max(jnp.abs(z), axis=1, keepdims=True)
            top = jnp.where(top > 1e-30, top, 1.0)
            code = jnp.round(z * (LEVELS / top)).astype(jnp.int32)
            wire[:, pl.ds(c * gw + h * hd, hd)] = code.astype(I16)
            steps.append(top * (1.0 / LEVELS))
        s_wire[c] = to_lanes(steps)

    def decode(c, ref, steps):
        tile = steps[c]
        return jnp.concatenate(
            [
                ref[:, pl.ds(c * gw + h * hd, hd)].astype(jnp.int32).astype(F32)
                * from_lanes(tile, h)
                for h in range(heads_of(c))
            ],
            axis=1,
        )

    def down(c):
        return remote(q_full.at[:, span_of(c)], q_full.at[:, span_of(c)], down_sem.at[c], "gx", outer)

    def o_up(c):
        return (
            remote(l_wire.at[c], l_end.at[c], l_up_sem.at[c], "gx", inner),
            remote(o_wire.at[c], o_end.at[c], o_up_sem.at[c], "gx", inner),
        )

    def o_over(c):
        return (
            remote(l_wire.at[c], l_mid.at[c], l_across_sem.at[c], "gx", other),
            remote(o_wire.at[c], o_mid.at[c], o_across_sem.at[c], "gx", other),
        )

    def o_down(c):
        return remote(
            att_full.at[:, span_of(c)], att_full.at[:, span_of(c)], o_down_sem.at[c], "gx", outer
        )

    def project(c):
        base = c * gw
        span = gw if c < groups else 2 * hd
        if c < groups:
            wq_copies[c].wait()
            wo_copies.append(
                load(out_weight.at[pl.ds(base, gw)], wo.at[pl.ds(base, gw)], 5 + groups + c)
            )
        else:
            wk_copy.wait()
            wv_copy.wait()

        w = wq[:, pl.ds(base, span)] if c < groups else wkv[...]
        y = jnp.dot(tok_full[...].reshape(total, -1), w, preferred_element_type=F32)

        @pl.when(mid)
        def _():
            part[:, pl.ds(base, span)] = y

        @pl.when(end)
        def _():
            encode(c, y)
            for copy in up(c):
                copy.start()

    def pass_on(c):
        @pl.when(mid)
        def _():
            for copy in up(c):
                copy.wait_recv()
            cols = span_of(c)
            y = part[:, cols] + decode(c, recv_end, s_end)
            part[:, cols] = y
            encode(c, y)
            for copy in over(c):
                copy.start()

    def settle(c):
        if c == groups:
            key_copy.wait()
            value_copy.wait()

        @pl.when(mid)
        def _():
            for copy in over(c):
                copy.wait_recv()
            cols = span_of(c)
            y = (part[:, cols] + decode(c, recv_mid, s_mid)).astype(BF)
            if c == groups:
                fresh[...] = y.reshape(2, half, 2 * hd)
                own = fresh[ix - 1]
                kbuf[pl.ds(cache_rows, half), :] = own[:, :hd]
                vbuf[pl.ds(cache_rows, half), :] = own[:, hd:]
            else:
                q_full[:, cols] = y
                down(c).start()

    tiles = [(a, min(512, cache_rows - a)) for a in range(0, cache_rows, 512)]
    tiles.append((cache_rows, 128))

    def attend(c):
        @pl.when(end)
        def _():
            down(c).wait_recv()

        q = jnp.concatenate(
            [
                q_full[:, pl.ds(c * gw + h * hd, hd)]
                for h in range(hpg)
            ],
            axis=0,
        )
        peak = jnp.full((hpg * total, 1), -1e20, F32)
        for a, t in tiles:
            s = lax.dot_general(
                q,
                kbuf[pl.ds(a, t), :],
                (((1,), (1,)), ((), ())),
                preferred_element_type=F32,
            )
            s = (s * scale).reshape(hpg, total, t) + bias[:, pl.ds(a, t)][None]
            s = s.reshape(hpg * total, t)
            scores[:, pl.ds(a, t)] = s
            peak = jnp.maximum(peak, jnp.max(s, axis=1, keepdims=True))
        acc = jnp.zeros((hpg * total, 2 * hd), F32)
        for a, t in tiles:
            p = jnp.exp2(scores[:, pl.ds(a, t)] - peak).astype(BF)
            v = jnp.concatenate([vbuf[pl.ds(a, t), :], vones[pl.ds(0, t), :]], axis=1)
            acc = acc + jnp.dot(p, v, preferred_element_type=F32)
        norm = acc[:, hd : hd + 1]
        some = norm > 0.0
        o = acc[:, :hd] / jnp.where(some, norm, 1.0)
        lse = jnp.where(some, peak + jnp.log2(jnp.where(some, norm, 1.0)), -1e20)
        parts = [slice(h * total, (h + 1) * total) for h in range(hpg)]
        tile = to_lanes([lse[rows] for rows in parts])
        wide = jnp.concatenate([o[rows] for rows in parts], axis=1)

        @pl.when(end)
        def _():
            l_wire[c] = tile
            o_wire[c] = wide.astype(BF)
            for copy in o_up(c):
                copy.start()

        @pl.when(mid)
        def _():
            l_part[c] = tile
            o_part[c] = wide

    def merged(c, o_ref, l_ref):
        mine, theirs = l_part[c], l_ref[c]
        top = jnp.maximum(mine, theirs)
        left, right = jnp.exp2(mine - top), jnp.exp2(theirs - top)
        both = left + right
        left, right = left / both, right / both
        pieces = []
        for h in range(hpg):
            cols = pl.ds(h * hd, hd)
            pieces.append(
                o_part[c, :, cols] * from_lanes(left, h)
                + o_ref[c, :, cols].astype(F32) * from_lanes(right, h)
            )
        return jnp.concatenate(pieces, axis=1), top + jnp.log2(both)

    def merge(c):
        @pl.when(mid)
        def _():
            for copy in o_up(c):
                copy.wait_recv()
            wide, tile = merged(c, o_end, l_end)
            l_part[c] = tile
            o_part[c] = wide
            l_wire[c] = tile
            o_wire[c] = wide.astype(BF)
            for copy in o_over(c):
                copy.start()

    def finish(c):
        @pl.when(mid)
        def _():
            for copy in o_over(c):
                copy.wait_recv()
            wide, _ = merged(c, o_mid, l_mid)
            att_full[:, span_of(c)] = wide.astype(BF)
            o_down(c).start()

    out_cols = out.shape[1]
    spans = 4
    sw = out_cols // spans

    def pair_copy(n):
        cols = pl.ds(n * sw, sw)
        return remote(
            o2_send.at[:, 1 - core, :, cols], recv3.at[:, :, cols], r3_sem.at[n], "gy", sibling
        )

    def cell_copy(n):
        cols = pl.ds(n * sw, sw)
        return remote(pair_sum.at[:, cols], recv4.at[:, cols], r4_sem.at[n], "gy", across)

    def pair(n):
        cols = pl.ds(n * sw, sw)
        pair_copy(n).wait_recv()
        y = o2_send[1 - cell, core, :, cols].astype(F32) + recv3[1 - cell, :, cols].astype(F32)
        pair_sum[:, cols] = y.astype(BF)
        cell_copy(n).start()


    def mix(c):
        @pl.when(end)
        def _():
            o_down(c).wait_recv()

        wo_copies[c].wait()
        last = c == groups - 1

        def columns(at):
            a = att_full[:, pl.ds(c * gw, gw)]
            y = jnp.dot(
                a, wo[pl.ds(c * gw, gw), pl.ds(at, TILE)], preferred_element_type=F32
            )
            if c > 0:
                y = y + macc[:, pl.ds(at, TILE)]
            if last:
                o2_send[:, :, :, pl.ds(at, TILE)] = y.astype(BF).reshape(2, 2, ROWS, TILE)
            else:
                macc[:, pl.ds(at, TILE)] = y

        if not last:

            @pl.loop(0, out_cols // TILE)
            def _(i):
                columns(pl.multiple_of(i * TILE, TILE))

            return
        for n in range(spans):

            @pl.loop(0, sw // TILE)
            def _(i):
                columns(pl.multiple_of(n * sw + i * TILE, TILE))

            pair_copy(n).start()
            if n > 0:
                pair(n - 1)
        pair(spans - 1)

    own_tokens.wait()
    tok_across.wait_recv()
    tok_relay = remote(tok_full.at[across], tok_full.at[across], tok_sem.at[2], "gy", sibling)
    tok_relay.start()
    tok_pair.wait_recv()
    tok_relay.wait_recv()
    steps = ('Pk', 'P0', 'P1', 'Xk', 'P2', 'X0', 'P3', 'X1', 'Yk', 'Y0', 'X2', 'Y1', 'X3', 'A0', 'Y2', 'A1', 'Y3', 'A2', 'A3', 'U0', 'U1', 'V0', 'U2', 'V1', 'U3', 'V2', 'M0', 'V3', 'M1', 'M2', 'M3')
    table = dict(P=project, X=pass_on, Y=settle, A=attend, U=merge, V=finish, M=mix)
    for step in steps:
        table[step[0]](groups if step[1] == "k" else int(step[1]))

    for n in range(spans):
        cols = pl.ds(n * sw, sw)
        y = o2_send[cell, core, :, cols].astype(F32) + recv3[cell, :, cols].astype(F32)
        cell_copy(n).wait_recv()
        out[:, cols] = (y + recv4[:, cols].astype(F32)).astype(BF)

    tok_across.wait_send()
    tok_pair.wait_send()
    tok_relay.wait_send()
    for n in range(spans):
        pair_copy(n).wait_send()
        cell_copy(n).wait_send()

    @pl.when(end)
    def _():
        for c in range(groups + 1):
            for copy in up(c):
                copy.wait_send()
        for c in range(groups):
            for copy in o_up(c):
                copy.wait_send()

    @pl.when(mid)
    def _():
        for c in range(groups + 1):
            for copy in over(c):
                copy.wait_send()
        for c in range(groups):
            down(c).wait_send()
            o_down(c).wait_send()
            for copy in o_over(c):
                copy.wait_send()


def fused_body(nx, ny, *args):
    tokens, q_weight, k_weight, v_weight, out_weight, cache_keys, cache_values, tenant_ids, prefix_len = args
    hd = cache_keys.shape[1]
    width = q_weight.shape[1]
    heads = width // hd
    groups = 4
    hpg = heads // groups
    gw = hpg * hd
    total = tenant_ids.shape[0]
    depth = tokens.shape[1]
    out_cols = out_weight.shape[1]
    rows = cache_keys.shape[0] + 128
    anywhere = pl.BlockSpec(memory_space=pl.ANY)
    vmem = pl.BlockSpec(memory_space=pltpu.VMEM)
    dma = pltpu.SemaphoreType.DMA
    chunks = groups + 1
    return pl.pallas_call(
        functools.partial(fused, nx, ny, heads, hd, hpg),
        out_shape=jax.ShapeDtypeStruct((ROWS, out_cols), BF),
        in_specs=[anywhere] * 7 + [vmem, pl.BlockSpec(memory_space=pltpu.SMEM)],
        out_specs=vmem,
        scratch_shapes=[
            pltpu.VMEM((ny, ROWS, depth), BF),
            pltpu.VMEM((depth, width), BF),
            pltpu.VMEM((depth, 2 * hd), BF),
            pltpu.VMEM((width, out_cols), BF),
            pltpu.VMEM((rows, hd), BF),
            pltpu.VMEM((rows, hd), BF),
            pltpu.VMEM((512, hd), BF),
            pltpu.VMEM((total, rows), F32),
            pltpu.VMEM((total, width + 2 * hd), F32),
            pltpu.VMEM((total, width + 2 * hd), I16),
            pltpu.VMEM((total, width + 2 * hd), I16),
            pltpu.VMEM((total, width + 2 * hd), I16),
            pltpu.VMEM((chunks, 8, 128), F32),
            pltpu.VMEM((chunks, 8, 128), F32),
            pltpu.VMEM((chunks, 8, 128), F32),
            pltpu.VMEM((2, total // 2, 2 * hd), BF),
            pltpu.VMEM((total, width), BF),
            pltpu.VMEM((hpg * total, rows), F32),
            pltpu.VMEM((groups, total, gw), F32),
            pltpu.VMEM((groups, 8, 128), F32),
            pltpu.VMEM((groups, total, gw), BF),
            pltpu.VMEM((groups, 8, 128), F32),
            pltpu.VMEM((groups, total, gw), BF),
            pltpu.VMEM((groups, 8, 128), F32),
            pltpu.VMEM((groups, total, gw), BF),
            pltpu.VMEM((groups, 8, 128), F32),
            pltpu.VMEM((total, width), BF),
            pltpu.VMEM((total, out_cols), F32),
            pltpu.VMEM((2, 2, ROWS, out_cols), BF),
            pltpu.VMEM((2, ROWS, out_cols), BF),
            pltpu.VMEM((ROWS, out_cols), BF),
            pltpu.VMEM((ROWS, out_cols), BF),
            dma((5 + 2 * groups,)),
            dma((3, 2)),
            dma((chunks, 2)),
            dma((chunks, 2)),
            dma((chunks, 2)),
            dma((chunks, 2)),
            dma((groups, 2)),
            dma((groups, 2)),
            dma((groups, 2)),
            dma((groups, 2)),
            dma((groups, 2)),
            dma((groups, 2)),
            dma((4, 2)),
            dma((4, 2)),
        ],
        compiler_params=pltpu.CompilerParams(
            collective_id=0, has_side_effects=True, vmem_limit_bytes=56 * 2**20
        ),
    )(
        tokens,
        q_weight,
        k_weight,
        v_weight,
        out_weight,
        cache_keys,
        cache_values,
        tenant_ids.reshape(1, total),
        prefix_len,
    )


def joined(part, axis, combine):
    gathered = jax.tree.map(lambda a: lax.all_gather(a, axis), part)

    def take(source):
        return jax.tree.map(lambda a: lax.dynamic_index_in_dim(a, source, 0, False), gathered)

    return lax.fori_loop(
        1, lax.axis_size(axis), lambda source, state: combine(state, take(source)), take(0)
    )


def combine_parts(left_part, right_part):
    left_peak, left_total, left_acc = left_part
    right_peak, right_total, right_acc = right_part
    joint_peak = jnp.maximum(left_peak, right_peak)
    left_factor = jnp.exp(left_peak - joint_peak)
    right_factor = jnp.exp(right_peak - joint_peak)
    joint_total = left_total * left_factor + right_total * right_factor
    joint_acc = left_acc * left_factor[..., None] + right_acc * right_factor[..., None]
    return (joint_peak, joint_total, joint_acc)


def body(
    tokens,
    q_weight,
    k_weight,
    v_weight,
    out_weight,
    cache_keys,
    cache_values,
    tenant_ids,
    prefix_len,
):
    head_dim = cache_keys.shape[1]
    q_width = q_weight.shape[1]
    head_group = q_width // head_dim
    total_tokens = tenant_ids.shape[0]
    own_rows = total_tokens // lax.axis_size("gx")
    gathered = lax.all_gather(tokens, "gy", axis=0, tiled=True)
    slab_rows = gathered
    projected = lax.psum_scatter(
        jnp.concatenate(
            [
                jnp.dot(slab_rows, q_weight, preferred_element_type=jnp.float32),
                jnp.dot(slab_rows, k_weight, preferred_element_type=jnp.float32),
                jnp.dot(slab_rows, v_weight, preferred_element_type=jnp.float32),
            ],
            axis=1,
        ),
        "gx",
        scatter_dimension=0,
        tiled=True,
    )
    own_queries = projected[:, :q_width].astype(jnp.bfloat16)
    new_keys = projected[:, q_width : q_width + head_dim].astype(jnp.bfloat16)
    new_values = projected[:, q_width + head_dim :].astype(jnp.bfloat16)
    queries = lax.all_gather(own_queries, "gx", axis=0, tiled=True)
    device_index = lax.axis_index("gx")
    tenant_count = prefix_len.shape[0]
    tenant_table = tenant_ids[:, None] == jnp.arange(tenant_count, dtype=jnp.int32)[None, :]
    prefix_of = jnp.sum(jnp.where(tenant_table, prefix_len[None, :], 0), axis=1)
    cache_rows = cache_keys.shape[0]
    key_pos = device_index * cache_rows + jnp.arange(cache_rows, dtype=jnp.int32)
    new_pos = device_index * own_rows + jnp.arange(own_rows, dtype=jnp.int32)
    new_tenant = lax.dynamic_slice_in_dim(tenant_ids, device_index * own_rows, own_rows, 0)
    block_tokens = math.gcd(total_tokens, max(1, 512 // head_group))
    score_scale = 1.0 / math.sqrt(head_dim)

    def attend_block(block_index):
        first_token = block_index * block_tokens
        q_rows = lax.dynamic_slice_in_dim(queries, first_token, block_tokens, 0).reshape(
            block_tokens * head_group, head_dim
        )
        rows_prefix = jnp.repeat(
            lax.dynamic_slice_in_dim(prefix_of, first_token, block_tokens, 0), head_group
        )
        rows_tenant = jnp.repeat(
            lax.dynamic_slice_in_dim(tenant_ids, first_token, block_tokens, 0), head_group
        )
        rows_pos = jnp.repeat(first_token + jnp.arange(block_tokens, dtype=jnp.int32), head_group)
        prefix_scores = (
            jnp.dot(q_rows, cache_keys.T, preferred_element_type=jnp.float32) * score_scale
        )
        allowed_prefix = key_pos[None, :] < rows_prefix[:, None]
        fresh_scores = jnp.dot(q_rows, new_keys.T, preferred_element_type=jnp.float32) * score_scale
        allowed_fresh = (new_tenant[None, :] == rows_tenant[:, None]) & (
            new_pos[None, :] <= rows_pos[:, None]
        )
        row_peak = jnp.maximum(
            jnp.max(jnp.where(allowed_prefix, prefix_scores, -1e30), axis=1),
            jnp.max(jnp.where(allowed_fresh, fresh_scores, -1e30), axis=1),
        )
        prefix_weights = jnp.where(
            allowed_prefix, jnp.exp(prefix_scores - row_peak[:, None]), 0.0
        ).astype(jnp.bfloat16)
        fresh_weights = jnp.where(
            allowed_fresh, jnp.exp(fresh_scores - row_peak[:, None]), 0.0
        ).astype(jnp.bfloat16)
        row_total = jnp.sum(prefix_weights.astype(jnp.float32), axis=1) + jnp.sum(
            fresh_weights.astype(jnp.float32), axis=1
        )
        row_acc = jnp.dot(prefix_weights, cache_values, preferred_element_type=jnp.float32)
        row_acc = row_acc + jnp.dot(fresh_weights, new_values, preferred_element_type=jnp.float32)
        return (
            row_peak.reshape(block_tokens, head_group),
            row_total.reshape(block_tokens, head_group),
            row_acc.reshape(block_tokens, head_group, head_dim),
        )

    peak_blocks, total_blocks, acc_blocks = lax.map(
        attend_block, jnp.arange(total_tokens // block_tokens, dtype=jnp.int32)
    )
    row_peaks = peak_blocks.reshape(total_tokens, head_group)
    row_totals = total_blocks.reshape(total_tokens, head_group)
    row_accs = acc_blocks.reshape(total_tokens, head_group, head_dim)
    joint_peak, joint_total, joint_acc = joined(
        (row_peaks, row_totals, row_accs), "gx", combine_parts
    )
    attended = (
        (joint_acc / joint_total[..., None]).astype(jnp.bfloat16).reshape(total_tokens, q_width)
    )
    slab_rows = attended
    mixed = lax.psum_scatter(
        jnp.dot(slab_rows, out_weight, preferred_element_type=jnp.float32),
        "gy",
        scatter_dimension=0,
        tiled=True,
    )
    return mixed.astype(jnp.bfloat16)


def solution(mesh):
    placed = (
        P(("groups", "gy"), "gx"),
        P("gx", "gy"),
        P("gx", "gy"),
        P("gx", "gy"),
        P("gy", "gx"),
        P(("groups", "gx"), "gy"),
        P(("groups", "gx"), "gy"),
        P("groups"),
        P("groups"),
    )
    nx, ny = mesh.shape["gx"], mesh.shape["gy"]

    def local(*args):
        whole = args[7].shape[0]
        if nx == ny == 4 and whole == nx * ROWS:
            return fused_body(nx, ny, *args)
        return body(*args)

    return jax.shard_map(
        local, mesh=mesh, in_specs=placed, out_specs=P(("groups", "gy"), "gx"), check_vma=False
    )
```

```python
import functools
import math

import jax
import jax.numpy as jnp
from jax import lax
from jax.experimental import pallas as pl
from jax.experimental.pallas import tpu as pltpu
from jax.sharding import PartitionSpec as P

BF = jnp.bfloat16
F32 = jnp.float32
I16 = jnp.int16
TILE = 1024
ROWS = 16
LEVELS = 32000.0


def fused(
    nx,
    ny,
    heads,
    hd,
    hpg,
    tokens,
    q_weight,
    k_weight,
    v_weight,
    out_weight,
    cache_keys,
    cache_values,
    tenants,
    prefix_len,
    out,
    tok_full,
    wq,
    wkv,
    wo,
    kbuf,
    vbuf,
    vones,
    bias,
    part,
    wire,
    recv_end,
    recv_mid,
    s_wire,
    s_end,
    s_mid,
    fresh,
    q_full,
    scores,
    o_part,
    l_part,
    o_wire,
    l_wire,
    o_end,
    l_end,
    o_mid,
    l_mid,
    att_full,
    macc,
    o2_send,
    recv3,
    pair_sum,
    recv4,
    load_sem,
    tok_sem,
    up_sem,
    across_sem,
    s_up_sem,
    s_across_sem,
    down_sem,
    o_up_sem,
    o_across_sem,
    l_up_sem,
    l_across_sem,
    o_down_sem,
    r3_sem,
    r4_sem,
):
    ix = lax.axis_index("gx")
    iy = lax.axis_index("gy")
    width = heads * hd
    groups = heads // hpg
    gw = hpg * hd
    total = nx * ROWS
    cache_rows = cache_keys.shape[0]
    scale = math.log2(math.e) / math.sqrt(hd)

    def load(src, dst, i):
        copy = pltpu.make_async_copy(src, dst, load_sem.at[i])
        copy.start()
        return copy

    end = (ix == 0) | (ix == nx - 1)
    mid = jnp.logical_not(end)
    inner = jnp.where(ix == 0, 1, nx - 2)
    outer = jnp.where(ix == 1, 0, nx - 1)
    other = nx - 1 - ix
    core = lax.rem(iy, 2)
    cell = iy // 2
    sibling = iy + 1 - 2 * core
    across = lax.rem(iy + 2, ny)

    def remote(src, dst, sems, axis, target):
        return pltpu.make_async_remote_copy(
            src_ref=src,
            dst_ref=dst,
            send_sem=sems.at[0],
            recv_sem=sems.at[1],
            device_id={axis: target},
            device_id_type=pl.DeviceIdType.MESH,
        )

    def signal(axis, target):
        pl.semaphore_signal(
            barrier, inc=1, device_id={axis: target}, device_id_type=pl.DeviceIdType.MESH
        )

    own_tokens = load(tokens, tok_full.at[iy], 0)
    wk_copy = load(k_weight, wkv.at[:, :hd], 1)
    wv_copy = load(v_weight, wkv.at[:, hd:], 2)
    wq_copies = [
        load(q_weight.at[:, pl.ds(c * gw, gw)], wq.at[:, pl.ds(c * gw, gw)], 3 + c)
        for c in range(groups)
    ]
    key_copy = load(cache_keys, kbuf.at[pl.ds(0, cache_rows)], 3 + groups)
    value_copy = load(cache_values, vbuf.at[pl.ds(0, cache_rows)], 4 + groups)

    barrier = pltpu.get_barrier_semaphore()
    signal("gy", sibling)
    signal("gy", across)

    @pl.when(end)
    def _():
        signal("gx", inner)
        pl.semaphore_wait(barrier, 3)

    @pl.when(mid)
    def _():
        signal("gx", outer)
        signal("gx", other)
        pl.semaphore_wait(barrier, 4)

    half_depth = tokens.shape[1] // 2
    halves = [pl.ds(0, half_depth), pl.ds(half_depth, half_depth)]
    tok_across = [
        remote(tokens.at[:, f], tok_full.at[iy, :, f], tok_sem.at[i], "gy", across)
        for i, f in enumerate(halves)
    ]
    for copy in tok_across:
        copy.start()
    tok_pair = remote(tokens, tok_full.at[iy], tok_sem.at[4], "gy", sibling)
    tok_pair.start()

    tid_row = tenants[...].astype(F32)
    r = lax.broadcasted_iota(jnp.int32, (total, total), 0)
    l = lax.broadcasted_iota(jnp.int32, (total, total), 1)
    tid = jnp.sum(
        jnp.where(r == l, jnp.broadcast_to(tid_row, (total, total)), 0.0), axis=1, keepdims=True
    )
    reach = jnp.zeros((total, 1), jnp.int32)
    for i in range(prefix_len.shape[0]):
        reach = jnp.where(tid == float(i), prefix_len[i], reach)
    pos = lax.broadcasted_iota(jnp.int32, (total, cache_rows), 1) + ix * cache_rows
    bias[:, pl.ds(0, cache_rows)] = jnp.where(pos < reach, 0.0, -1e30)
    row = lax.broadcasted_iota(jnp.int32, (total, 128), 0)
    lane = lax.broadcasted_iota(jnp.int32, (total, 128), 1)
    half = total // 2
    new = lane + (ix - 1) * half
    new_tid = jnp.sum(jnp.where(row == new, tid, 0.0), axis=0, keepdims=True)
    ok = (new_tid == tid) & (new <= row) & (lane < half) & (new >= 0)
    bias[:, pl.ds(cache_rows, 128)] = jnp.where(ok, 0.0, -1e30)
    vones[...] = jnp.ones_like(vones)
    kbuf[pl.ds(cache_rows, 128), :] = jnp.zeros((128, hd), BF)
    vbuf[pl.ds(cache_rows, 128), :] = jnp.zeros((128, hd), BF)

    wo_copies = []
    eye = row == lane
    level = lax.broadcasted_iota(jnp.int32, (8, 128), 0)

    def to_lanes(columns):
        tile = jnp.zeros((8, 128), F32)
        for h, column in enumerate(columns):
            flat = jnp.sum(jnp.where(eye, column, 0.0), axis=0, keepdims=True)
            tile = jnp.where(level == h, flat, tile)
        return tile

    def from_lanes(tile, h):
        return jnp.sum(jnp.where(eye, tile[h : h + 1, :], 0.0), axis=1, keepdims=True)

    def span_of(c):
        return pl.ds(c * gw, gw if c < groups else 2 * hd)

    def up(c):
        return (
            remote(s_wire.at[c], s_end.at[c], s_up_sem.at[c], "gx", inner),
            remote(wire.at[:, span_of(c)], recv_end.at[:, span_of(c)], up_sem.at[c], "gx", inner),
        )

    def over(c):
        return (
            remote(s_wire.at[c], s_mid.at[c], s_across_sem.at[c], "gx", other),
            remote(
                wire.at[:, span_of(c)], recv_mid.at[:, span_of(c)], across_sem.at[c], "gx", other
            ),
        )

    def heads_of(c):
        return hpg if c < groups else 2

    def encode(c, y):
        steps = []
        for h in range(heads_of(c)):
            z = y[:, h * hd : (h + 1) * hd]
            top = jnp.max(jnp.abs(z), axis=1, keepdims=True)
            top = jnp.where(top > 1e-30, top, 1.0)
            code = jnp.round(z * (LEVELS / top)).astype(jnp.int32)
            wire[:, pl.ds(c * gw + h * hd, hd)] = code.astype(I16)
            steps.append(top * (1.0 / LEVELS))
        s_wire[c] = to_lanes(steps)

    def decode(c, ref, steps):
        tile = steps[c]
        return jnp.concatenate(
            [
                ref[:, pl.ds(c * gw + h * hd, hd)].astype(jnp.int32).astype(F32)
                * from_lanes(tile, h)
                for h in range(heads_of(c))
            ],
            axis=1,
        )

    def down(c):
        return remote(q_full.at[:, span_of(c)], q_full.at[:, span_of(c)], down_sem.at[c], "gx", outer)

    def o_up(c):
        return (
            remote(l_wire.at[c], l_end.at[c], l_up_sem.at[c], "gx", inner),
            remote(o_wire.at[c], o_end.at[c], o_up_sem.at[c], "gx", inner),
        )

    def o_over(c):
        return (
            remote(l_wire.at[c], l_mid.at[c], l_across_sem.at[c], "gx", other),
            remote(o_wire.at[c], o_mid.at[c], o_across_sem.at[c], "gx", other),
        )

    def o_down(c):
        return remote(
            att_full.at[:, span_of(c)], att_full.at[:, span_of(c)], o_down_sem.at[c], "gx", outer
        )

    def project(c):
        base = c * gw
        span = gw if c < groups else 2 * hd
        if c < groups:
            wq_copies[c].wait()
            wo_copies.append(
                load(out_weight.at[pl.ds(base, gw)], wo.at[pl.ds(base, gw)], 5 + groups + c)
            )
        else:
            wk_copy.wait()
            wv_copy.wait()

        w = wq[:, pl.ds(base, span)] if c < groups else wkv[...]
        y = jnp.dot(tok_full[...].reshape(total, -1), w, preferred_element_type=F32)

        @pl.when(mid)
        def _():
            part[:, pl.ds(base, span)] = y

        @pl.when(end)
        def _():
            encode(c, y)
            for copy in up(c):
                copy.start()

    def pass_on(c):
        @pl.when(mid)
        def _():
            for copy in up(c):
                copy.wait_recv()
            cols = span_of(c)
            y = part[:, cols] + decode(c, recv_end, s_end)
            part[:, cols] = y
            encode(c, y)
            for copy in over(c):
                copy.start()

    def settle(c):
        if c == groups:
            key_copy.wait()
            value_copy.wait()

        @pl.when(mid)
        def _():
            for copy in over(c):
                copy.wait_recv()
            cols = span_of(c)
            y = (part[:, cols] + decode(c, recv_mid, s_mid)).astype(BF)
            if c == groups:
                fresh[...] = y.reshape(2, half, 2 * hd)
                own = fresh[ix - 1]
                kbuf[pl.ds(cache_rows, half), :] = own[:, :hd]
                vbuf[pl.ds(cache_rows, half), :] = own[:, hd:]
            else:
                q_full[:, cols] = y
                down(c).start()

    tiles = [(a, min(512, cache_rows - a)) for a in range(0, cache_rows, 512)]
    tiles.append((cache_rows, 128))

    def attend(c):
        @pl.when(end)
        def _():
            down(c).wait_recv()

        q = jnp.concatenate(
            [
                q_full[:, pl.ds(c * gw + h * hd, hd)]
                for h in range(hpg)
            ],
            axis=0,
        )
        peak = jnp.full((hpg * total, 1), -1e20, F32)
        for a, t in tiles:
            s = lax.dot_general(
                q,
                kbuf[pl.ds(a, t), :],
                (((1,), (1,)), ((), ())),
                preferred_element_type=F32,
            )
            s = (s * scale).reshape(hpg, total, t) + bias[:, pl.ds(a, t)][None]
            s = s.reshape(hpg * total, t)
            scores[:, pl.ds(a, t)] = s
            peak = jnp.maximum(peak, jnp.max(s, axis=1, keepdims=True))
        acc = jnp.zeros((hpg * total, 2 * hd), F32)
        for a, t in tiles:
            p = jnp.exp2(scores[:, pl.ds(a, t)] - peak).astype(BF)
            v = jnp.concatenate([vbuf[pl.ds(a, t), :], vones[pl.ds(0, t), :]], axis=1)
            acc = acc + jnp.dot(p, v, preferred_element_type=F32)
        norm = acc[:, hd : hd + 1]
        some = norm > 0.0
        o = acc[:, :hd] / jnp.where(some, norm, 1.0)
        lse = jnp.where(some, peak + jnp.log2(jnp.where(some, norm, 1.0)), -1e20)
        parts = [slice(h * total, (h + 1) * total) for h in range(hpg)]
        tile = to_lanes([lse[rows] for rows in parts])
        wide = jnp.concatenate([o[rows] for rows in parts], axis=1)

        @pl.when(end)
        def _():
            l_wire[c] = tile
            o_wire[c] = wide.astype(BF)
            for copy in o_up(c):
                copy.start()

        @pl.when(mid)
        def _():
            l_part[c] = tile
            o_part[c] = wide

    def merged(c, o_ref, l_ref):
        mine, theirs = l_part[c], l_ref[c]
        top = jnp.maximum(mine, theirs)
        left, right = jnp.exp2(mine - top), jnp.exp2(theirs - top)
        both = left + right
        left, right = left / both, right / both
        pieces = []
        for h in range(hpg):
            cols = pl.ds(h * hd, hd)
            pieces.append(
                o_part[c, :, cols] * from_lanes(left, h)
                + o_ref[c, :, cols].astype(F32) * from_lanes(right, h)
            )
        return jnp.concatenate(pieces, axis=1), top + jnp.log2(both)

    def merge(c):
        @pl.when(mid)
        def _():
            for copy in o_up(c):
                copy.wait_recv()
            wide, tile = merged(c, o_end, l_end)
            l_part[c] = tile
            o_part[c] = wide
            l_wire[c] = tile
            o_wire[c] = wide.astype(BF)
            for copy in o_over(c):
                copy.start()

    def finish(c):
        @pl.when(mid)
        def _():
            for copy in o_over(c):
                copy.wait_recv()
            wide, _ = merged(c, o_mid, l_mid)
            att_full[:, span_of(c)] = wide.astype(BF)
            o_down(c).start()

    out_cols = out.shape[1]
    spans = 4
    sw = out_cols // spans

    def pair_copy(n):
        cols = pl.ds(n * sw, sw)
        return remote(
            o2_send.at[:, 1 - core, :, cols], recv3.at[:, :, cols], r3_sem.at[n], "gy", sibling
        )

    def cell_copy(n):
        cols = pl.ds(n * sw, sw)
        return remote(pair_sum.at[:, cols], recv4.at[:, cols], r4_sem.at[n], "gy", across)

    def pair(n):
        cols = pl.ds(n * sw, sw)
        pair_copy(n).wait_recv()
        y = o2_send[1 - cell, core, :, cols].astype(F32) + recv3[1 - cell, :, cols].astype(F32)
        pair_sum[:, cols] = y.astype(BF)
        cell_copy(n).start()


    def mix(c):
        @pl.when(end)
        def _():
            o_down(c).wait_recv()

        wo_copies[c].wait()
        last = c == groups - 1

        def columns(at):
            a = att_full[:, pl.ds(c * gw, gw)]
            y = jnp.dot(
                a, wo[pl.ds(c * gw, gw), pl.ds(at, TILE)], preferred_element_type=F32
            )
            if c > 0:
                y = y + macc[:, pl.ds(at, TILE)]
            if last:
                o2_send[:, :, :, pl.ds(at, TILE)] = y.astype(BF).reshape(2, 2, ROWS, TILE)
            else:
                macc[:, pl.ds(at, TILE)] = y

        if not last:

            @pl.loop(0, out_cols // TILE)
            def _(i):
                columns(pl.multiple_of(i * TILE, TILE))

            return
        for n in range(spans):

            @pl.loop(0, sw // TILE)
            def _(i):
                columns(pl.multiple_of(n * sw + i * TILE, TILE))

            pair_copy(n).start()
            if n > 0:
                pair(n - 1)
        pair(spans - 1)

    own_tokens.wait()
    tok_relay = []
    for i, f in enumerate(halves):
        tok_across[i].wait_recv()
        block = tok_full.at[across, :, f]
        tok_relay.append(remote(block, block, tok_sem.at[2 + i], "gy", sibling))
        tok_relay[i].start()
    tok_pair.wait_recv()
    for copy in tok_relay:
        copy.wait_recv()
    steps = ('Pk', 'P0', 'P1', 'Xk', 'P2', 'X0', 'P3', 'X1', 'Yk', 'Y0', 'X2', 'Y1', 'X3', 'A0', 'Y2', 'A1', 'Y3', 'A2', 'A3', 'U0', 'U1', 'V0', 'U2', 'V1', 'U3', 'V2', 'V3', 'M0', 'M1', 'M2', 'M3')
    table = dict(P=project, X=pass_on, Y=settle, A=attend, U=merge, V=finish, M=mix)
    for step in steps:
        table[step[0]](groups if step[1] == "k" else int(step[1]))

    for n in range(spans):
        cols = pl.ds(n * sw, sw)
        y = o2_send[cell, core, :, cols].astype(F32) + recv3[cell, :, cols].astype(F32)
        cell_copy(n).wait_recv()
        out[:, cols] = (y + recv4[:, cols].astype(F32)).astype(BF)

    tok_pair.wait_send()
    for copy in tok_across + tok_relay:
        copy.wait_send()
    for n in range(spans):
        pair_copy(n).wait_send()
        cell_copy(n).wait_send()

    @pl.when(end)
    def _():
        for c in range(groups + 1):
            for copy in up(c):
                copy.wait_send()
        for c in range(groups):
            for copy in o_up(c):
                copy.wait_send()

    @pl.when(mid)
    def _():
        for c in range(groups + 1):
            for copy in over(c):
                copy.wait_send()
        for c in range(groups):
            down(c).wait_send()
            o_down(c).wait_send()
            for copy in o_over(c):
                copy.wait_send()


def fused_body(nx, ny, *args):
    tokens, q_weight, k_weight, v_weight, out_weight, cache_keys, cache_values, tenant_ids, prefix_len = args
    hd = cache_keys.shape[1]
    width = q_weight.shape[1]
    heads = width // hd
    groups = 4
    hpg = heads // groups
    gw = hpg * hd
    total = tenant_ids.shape[0]
    depth = tokens.shape[1]
    out_cols = out_weight.shape[1]
    rows = cache_keys.shape[0] + 128
    anywhere = pl.BlockSpec(memory_space=pl.ANY)
    vmem = pl.BlockSpec(memory_space=pltpu.VMEM)
    dma = pltpu.SemaphoreType.DMA
    chunks = groups + 1
    return pl.pallas_call(
        functools.partial(fused, nx, ny, heads, hd, hpg),
        out_shape=jax.ShapeDtypeStruct((ROWS, out_cols), BF),
        in_specs=[anywhere] * 7 + [vmem, pl.BlockSpec(memory_space=pltpu.SMEM)],
        out_specs=vmem,
        scratch_shapes=[
            pltpu.VMEM((ny, ROWS, depth), BF),
            pltpu.VMEM((depth, width), BF),
            pltpu.VMEM((depth, 2 * hd), BF),
            pltpu.VMEM((width, out_cols), BF),
            pltpu.VMEM((rows, hd), BF),
            pltpu.VMEM((rows, hd), BF),
            pltpu.VMEM((512, hd), BF),
            pltpu.VMEM((total, rows), F32),
            pltpu.VMEM((total, width + 2 * hd), F32),
            pltpu.VMEM((total, width + 2 * hd), I16),
            pltpu.VMEM((total, width + 2 * hd), I16),
            pltpu.VMEM((total, width + 2 * hd), I16),
            pltpu.VMEM((chunks, 8, 128), F32),
            pltpu.VMEM((chunks, 8, 128), F32),
            pltpu.VMEM((chunks, 8, 128), F32),
            pltpu.VMEM((2, total // 2, 2 * hd), BF),
            pltpu.VMEM((total, width), BF),
            pltpu.VMEM((hpg * total, rows), F32),
            pltpu.VMEM((groups, total, gw), F32),
            pltpu.VMEM((groups, 8, 128), F32),
            pltpu.VMEM((groups, total, gw), BF),
            pltpu.VMEM((groups, 8, 128), F32),
            pltpu.VMEM((groups, total, gw), BF),
            pltpu.VMEM((groups, 8, 128), F32),
            pltpu.VMEM((groups, total, gw), BF),
            pltpu.VMEM((groups, 8, 128), F32),
            pltpu.VMEM((total, width), BF),
            pltpu.VMEM((total, out_cols), F32),
            pltpu.VMEM((2, 2, ROWS, out_cols), BF),
            pltpu.VMEM((2, ROWS, out_cols), BF),
            pltpu.VMEM((ROWS, out_cols), BF),
            pltpu.VMEM((ROWS, out_cols), BF),
            dma((5 + 2 * groups,)),
            dma((5, 2)),
            dma((chunks, 2)),
            dma((chunks, 2)),
            dma((chunks, 2)),
            dma((chunks, 2)),
            dma((groups, 2)),
            dma((groups, 2)),
            dma((groups, 2)),
            dma((groups, 2)),
            dma((groups, 2)),
            dma((groups, 2)),
            dma((4, 2)),
            dma((4, 2)),
        ],
        compiler_params=pltpu.CompilerParams(
            collective_id=0, has_side_effects=True, vmem_limit_bytes=56 * 2**20
        ),
    )(
        tokens,
        q_weight,
        k_weight,
        v_weight,
        out_weight,
        cache_keys,
        cache_values,
        tenant_ids.reshape(1, total),
        prefix_len,
    )


def joined(part, axis, combine):
    gathered = jax.tree.map(lambda a: lax.all_gather(a, axis), part)

    def take(source):
        return jax.tree.map(lambda a: lax.dynamic_index_in_dim(a, source, 0, False), gathered)

    return lax.fori_loop(
        1, lax.axis_size(axis), lambda source, state: combine(state, take(source)), take(0)
    )


def combine_parts(left_part, right_part):
    left_peak, left_total, left_acc = left_part
    right_peak, right_total, right_acc = right_part
    joint_peak = jnp.maximum(left_peak, right_peak)
    left_factor = jnp.exp(left_peak - joint_peak)
    right_factor = jnp.exp(right_peak - joint_peak)
    joint_total = left_total * left_factor + right_total * right_factor
    joint_acc = left_acc * left_factor[..., None] + right_acc * right_factor[..., None]
    return (joint_peak, joint_total, joint_acc)


def body(
    tokens,
    q_weight,
    k_weight,
    v_weight,
    out_weight,
    cache_keys,
    cache_values,
    tenant_ids,
    prefix_len,
):
    head_dim = cache_keys.shape[1]
    q_width = q_weight.shape[1]
    head_group = q_width // head_dim
    total_tokens = tenant_ids.shape[0]
    own_rows = total_tokens // lax.axis_size("gx")
    gathered = lax.all_gather(tokens, "gy", axis=0, tiled=True)
    slab_rows = gathered
    projected = lax.psum_scatter(
        jnp.concatenate(
            [
                jnp.dot(slab_rows, q_weight, preferred_element_type=jnp.float32),
                jnp.dot(slab_rows, k_weight, preferred_element_type=jnp.float32),
                jnp.dot(slab_rows, v_weight, preferred_element_type=jnp.float32),
            ],
            axis=1,
        ),
        "gx",
        scatter_dimension=0,
        tiled=True,
    )
    own_queries = projected[:, :q_width].astype(jnp.bfloat16)
    new_keys = projected[:, q_width : q_width + head_dim].astype(jnp.bfloat16)
    new_values = projected[:, q_width + head_dim :].astype(jnp.bfloat16)
    queries = lax.all_gather(own_queries, "gx", axis=0, tiled=True)
    device_index = lax.axis_index("gx")
    tenant_count = prefix_len.shape[0]
    tenant_table = tenant_ids[:, None] == jnp.arange(tenant_count, dtype=jnp.int32)[None, :]
    prefix_of = jnp.sum(jnp.where(tenant_table, prefix_len[None, :], 0), axis=1)
    cache_rows = cache_keys.shape[0]
    key_pos = device_index * cache_rows + jnp.arange(cache_rows, dtype=jnp.int32)
    new_pos = device_index * own_rows + jnp.arange(own_rows, dtype=jnp.int32)
    new_tenant = lax.dynamic_slice_in_dim(tenant_ids, device_index * own_rows, own_rows, 0)
    block_tokens = math.gcd(total_tokens, max(1, 512 // head_group))
    score_scale = 1.0 / math.sqrt(head_dim)

    def attend_block(block_index):
        first_token = block_index * block_tokens
        q_rows = lax.dynamic_slice_in_dim(queries, first_token, block_tokens, 0).reshape(
            block_tokens * head_group, head_dim
        )
        rows_prefix = jnp.repeat(
            lax.dynamic_slice_in_dim(prefix_of, first_token, block_tokens, 0), head_group
        )
        rows_tenant = jnp.repeat(
            lax.dynamic_slice_in_dim(tenant_ids, first_token, block_tokens, 0), head_group
        )
        rows_pos = jnp.repeat(first_token + jnp.arange(block_tokens, dtype=jnp.int32), head_group)
        prefix_scores = (
            jnp.dot(q_rows, cache_keys.T, preferred_element_type=jnp.float32) * score_scale
        )
        allowed_prefix = key_pos[None, :] < rows_prefix[:, None]
        fresh_scores = jnp.dot(q_rows, new_keys.T, preferred_element_type=jnp.float32) * score_scale
        allowed_fresh = (new_tenant[None, :] == rows_tenant[:, None]) & (
            new_pos[None, :] <= rows_pos[:, None]
        )
        row_peak = jnp.maximum(
            jnp.max(jnp.where(allowed_prefix, prefix_scores, -1e30), axis=1),
            jnp.max(jnp.where(allowed_fresh, fresh_scores, -1e30), axis=1),
        )
        prefix_weights = jnp.where(
            allowed_prefix, jnp.exp(prefix_scores - row_peak[:, None]), 0.0
        ).astype(jnp.bfloat16)
        fresh_weights = jnp.where(
            allowed_fresh, jnp.exp(fresh_scores - row_peak[:, None]), 0.0
        ).astype(jnp.bfloat16)
        row_total = jnp.sum(prefix_weights.astype(jnp.float32), axis=1) + jnp.sum(
            fresh_weights.astype(jnp.float32), axis=1
        )
        row_acc = jnp.dot(prefix_weights, cache_values, preferred_element_type=jnp.float32)
        row_acc = row_acc + jnp.dot(fresh_weights, new_values, preferred_element_type=jnp.float32)
        return (
            row_peak.reshape(block_tokens, head_group),
            row_total.reshape(block_tokens, head_group),
            row_acc.reshape(block_tokens, head_group, head_dim),
        )

    peak_blocks, total_blocks, acc_blocks = lax.map(
        attend_block, jnp.arange(total_tokens // block_tokens, dtype=jnp.int32)
    )
    row_peaks = peak_blocks.reshape(total_tokens, head_group)
    row_totals = total_blocks.reshape(total_tokens, head_group)
    row_accs = acc_blocks.reshape(total_tokens, head_group, head_dim)
    joint_peak, joint_total, joint_acc = joined(
        (row_peaks, row_totals, row_accs), "gx", combine_parts
    )
    attended = (
        (joint_acc / joint_total[..., None]).astype(jnp.bfloat16).reshape(total_tokens, q_width)
    )
    slab_rows = attended
    mixed = lax.psum_scatter(
        jnp.dot(slab_rows, out_weight, preferred_element_type=jnp.float32),
        "gy",
        scatter_dimension=0,
        tiled=True,
    )
    return mixed.astype(jnp.bfloat16)


def solution(mesh):
    placed = (
        P(("groups", "gy"), "gx"),
        P("gx", "gy"),
        P("gx", "gy"),
        P("gx", "gy"),
        P("gy", "gx"),
        P(("groups", "gx"), "gy"),
        P(("groups", "gx"), "gy"),
        P("groups"),
        P("groups"),
    )
    nx, ny = mesh.shape["gx"], mesh.shape["gy"]

    def local(*args):
        whole = args[7].shape[0]
        if nx == ny == 4 and whole == nx * ROWS:
            return fused_body(nx, ny, *args)
        return body(*args)

    return jax.shard_map(
        local, mesh=mesh, in_specs=placed, out_specs=P(("groups", "gy"), "gx"), check_vma=False
    )
```
